512 devices in a mesh: ctx: 16 (over x, y), sp: 32 (over z, core).
Axes of the slice: x: 4, y: 4, z: 16, core: 2. Of those that a mesh axis runs over, the one named last changes fastest.
Arguments:
- queries: bfloat16 [65536, 4096], P(('ctx', 'sp')), may hold values from -6 to 6
- keys: bfloat16 [65536, 4096], P(('ctx', 'sp')), may hold values from -6 to 6
- out_grad: bfloat16 [65536, 4096], P(('ctx', 'sp')), may hold values from -2.5 to 2.5
- log_decay: bfloat16 [65536, 32], P(('ctx', 'sp')), may hold values from -0.75 to 0, as said below
Outputs:
- value_grad: bfloat16 [65536, 4096], P(('ctx', 'sp'))
The draws below stay inside these ranges and needn't reach their ends.
Inputs may be any that keep to these rules, and one draw needn't show every extreme that they name: `log_decay`: every entry is negative.
All inputs are finite; a program needn't handle non-finite values.
Results may differ from the reference program's by a relative error of at most 0.001.
Values may be sent and summed in bfloat16 or wider, within the bound.
A program may use at most 64 MiB of HBM per device.

```python
import math
import jax
import jax.numpy as jnp
from jax import lax

HEAD_GROUP = 32
HEAD_DIM = 128
BLOCK = 512
TOK_DEV = 128
TOKEN_COUNT = 65536


def draw_log_decay(key, part):
    key = jax.random.fold_in(key, 11)
    random_subkeys = jax.random.split(key, 7)
    slow_share = 5
    slow_heads = jax.random.randint(random_subkeys[0], (HEAD_GROUP,), 0, 10) < slow_share
    fast_rate = jnp.exp(jax.random.uniform(random_subkeys[1], (HEAD_GROUP,), minval=math.log(1.0 / 50.0), maxval=math.log(1.0 / 30.0)))
    slow_rate = jnp.exp(jax.random.uniform(random_subkeys[2], (HEAD_GROUP,), minval=math.log(0.1), maxval=math.log(0.6))) / TOKEN_COUNT
    head_rate = jnp.where(slow_heads, slow_rate, fast_rate)
    device_factor = jnp.exp(jax.random.uniform(random_subkeys[3], (TOKEN_COUNT // TOK_DEV, HEAD_GROUP), minval=math.log(0.5), maxval=math.log(2.0)))
    device_factor = jnp.repeat(device_factor, TOK_DEV, axis=0)
    token_factor = jnp.exp(jax.random.uniform(random_subkeys[4], (TOKEN_COUNT, HEAD_GROUP), minval=math.log(0.6), maxval=math.log(1.6)))
    decay_rates = head_rate[None, :] * device_factor * token_factor
    spike_row_list = jax.random.randint(random_subkeys[5], (2,), 0, TOKEN_COUNT)
    token_positions = jnp.arange(TOKEN_COUNT)
    spike_selected = jnp.any(token_positions[:, None] == spike_row_list[None, :], axis=1)
    spike_dropped = jax.random.uniform(random_subkeys[6], (HEAD_GROUP,), minval=0.2, maxval=0.4)
    log_recorded = -decay_rates + jnp.where(spike_selected[:, None], jnp.log1p(-spike_dropped)[None, :], 0.0)
    return log_recorded.astype(jnp.bfloat16)


def levels(stream_key, extent, cuts, low, largest):
    factor_of = 1.0
    for axis_at, parts in cuts:
        steps = jax.random.uniform(jax.random.fold_in(jax.random.fold_in(stream_key, 6), axis_at), (parts,), jnp.float32, low / len(cuts), largest / len(cuts))
        factor_of = factor_of * jnp.repeat(jnp.exp(steps), extent[axis_at] // parts).reshape((-1,) + (1,) * (len(extent) - 1 - axis_at))
    return factor_of


def bell_draw(key, shape, spread, limit, cuts=(), kind=jnp.bfloat16):
    entries = jax.random.normal(key, shape, jnp.float32) * spread
    if len(cuts) > 0:
        entries = levels(key, shape, cuts, -0.22, 0.18) * entries
    return jnp.clip(entries, min=-limit, max=limit).astype(kind)


def setup_inputs(seed: int = 0) -> dict:
    seeds = jax.random.split(jax.random.key(seed), 5)
    queries = bell_draw(seeds[0], (TOKEN_COUNT, HEAD_GROUP * HEAD_DIM), 1.0, 6.0, ((0, 512),))
    keys = bell_draw(seeds[1], (TOKEN_COUNT, HEAD_GROUP * HEAD_DIM), 1.0, 6.0, ((0, 512),))
    out_grad = bell_draw(seeds[2], (TOKEN_COUNT, HEAD_GROUP * HEAD_DIM), 0.25, 2.5, ((0, 512),))
    log_decay = draw_log_decay(jax.random.fold_in(seeds[4], 71), 0)
    return {"queries": queries, "keys": keys, "out_grad": out_grad, "log_decay": log_decay}


def block_grads(carried_state, pieces):
    query_blk, key_blk, grad_blk, log_cum = pieces
    exact = lax.Precision.HIGHEST
    query_f = query_blk.astype(jnp.float32)
    key_f = key_blk.astype(jnp.float32)
    grad_f = grad_blk.astype(jnp.float32)
    block_total = log_cum[-1]
    scores = jnp.einsum("shd,thd->hst", key_f, query_f, precision=exact) * (1.0 / HEAD_DIM)
    log_gaps = log_cum.T[:, None, :] - log_cum.T[:, :, None]
    token_positions = jnp.arange(log_cum.shape[0])
    upper_mask = token_positions[None, :] >= token_positions[:, None]
    decay_table = jnp.where(upper_mask, jnp.exp(jnp.where(upper_mask, log_gaps, 0.0)), 0.0)
    block_weights = (scores * decay_table).astype(jnp.bfloat16)
    inside = jnp.einsum("hst,thd->shd", block_weights.astype(jnp.float32), grad_f, precision=exact)
    to_end = jnp.exp(block_total[None, :] - log_cum)
    carried_term = jnp.einsum("shd,hde->she", key_f * to_end[:, :, None], carried_state, precision=exact)
    query_scaled = query_f * jnp.exp(log_cum)[:, :, None]
    new_state = jnp.exp(block_total)[:, None, None] * carried_state + jnp.einsum("thd,the->hde", query_scaled, grad_f, precision=exact)
    return new_state, (inside + carried_term).astype(jnp.bfloat16)


def reference(queries, keys, out_grad, log_decay):
    total_rows = queries.shape[0]
    block_count = total_rows // BLOCK
    shaped = (block_count, BLOCK, HEAD_GROUP, HEAD_DIM)
    log_cum = jnp.cumsum(log_decay.astype(jnp.float32).reshape(block_count, BLOCK, HEAD_GROUP), axis=1)
    start_state = jnp.zeros((HEAD_GROUP, HEAD_DIM, HEAD_DIM), jnp.float32)
    final_state, value_blocks = lax.scan(block_grads, start_state, (queries.reshape(shaped), keys.reshape(shaped), out_grad.reshape(shaped), log_cum), reverse=True)
    return value_blocks.reshape(total_rows, HEAD_GROUP * HEAD_DIM)
```

```python
import functools

import jax
import jax.numpy as jnp
from jax import lax
from jax.experimental import pallas as pl
from jax.experimental.pallas import tpu as pltpu
from jax.sharding import PartitionSpec as P

HEAD_DIM = 128
MESH = pl.DeviceIdType.MESH
F32 = jnp.float32
BF16 = jnp.bfloat16
SPLIT = 2
HOP = 3
KC, KF, KH, KZF, KZH, KS = range(6)
WX, WY, WH, WA, WZ, WZH, WU = range(7)


def dot(a, b, contract):
    return lax.dot_general(a, b, (contract, ((), ())), preferred_element_type=F32)


def kernel(dims, *refs):
    nx, ny, nz, heads, tok = dims
    nc = nx * ny
    (q_hbm, k_hbm, g_hbm, ld_hbm, out_hbm, qv, kv, gv, ldv, cum_b, cum_t, zl, ps, wt, states, c_out, f_out, h_out, zf_out,
     zh_out, c_in, f_in, h_in, zf_in, zh_in, s_in, a_plus, inside, out_v, in_local, in_send, in_recv, zl_send, zl_recv,
     ps_send, ps_recv, st_send, st_recv, o_local, o_send, o_recv) = refs
    pieces = heads * SPLIT
    rows = HEAD_DIM // SPLIT
    cols = heads * HEAD_DIM
    both = 2 * tok
    c = lax.axis_index("ctx")
    s = lax.axis_index("sp")
    x, y = lax.div(c, ny), lax.rem(c, ny)
    z, core = lax.div(s, 2), lax.rem(s, 2)
    peer = (c, z * 2 + 1 - core)

    def at_z(k):
        return (c, lax.rem(z + k + nz, nz) * 2 + core)

    def at_c(k):
        return (lax.rem(c + k + nc, nc), s)

    mine = pl.ds(pl.multiple_of(core * tok, tok), tok)
    other = pl.ds(pl.multiple_of((1 - core) * tok, tok), tok)
    my_cols = pl.ds(pl.multiple_of(core * cols, cols), cols)
    peer_cols = pl.ds(pl.multiple_of((1 - core) * cols, cols), cols)

    ins = ((q_hbm, qv), (g_hbm, gv), (k_hbm, kv))
    local = [pltpu.make_async_copy(ld_hbm, ldv.at[mine], in_local.at[3])]
    for j, (src, dst) in enumerate(ins):
        local.append(pltpu.make_async_copy(src.at[:, my_cols], dst.at[mine], in_local.at[j]))
    for copy in local:
        copy.start()

    barrier = pltpu.get_barrier_semaphore()
    friends = [peer] + [at_z(k) for k in range(1, nz)] + [at_c(k) for k in range(1, ny + 1)] + [
        at_c(-k) for k in range(1, ny + 1)
    ]
    for friend in friends:
        pl.semaphore_signal(barrier, inc=1, device_id=friend, device_id_type=MESH)
    pl.semaphore_wait(barrier, len(friends))

    def remote(src, dst, send, recv, to):
        return pltpu.make_async_remote_copy(
            src_ref=src, dst_ref=dst, send_sem=send, recv_sem=recv, device_id=to, device_id_type=MESH
        )

    swaps = [remote(ld_hbm, ldv.at[mine], in_send.at[3], in_recv.at[3], peer)]
    for j, (src, dst) in enumerate(ins):
        swaps.append(remote(src.at[:, peer_cols], dst.at[mine], in_send.at[j], in_recv.at[j], peer))
    for copy in swaps:
        copy.start()

    def clear(ref):
        ref[...] = jnp.zeros(ref.shape, ref.dtype)

    pl.when(x == nx - 1)(lambda: clear(c_in))
    pl.when(y == ny - 1)(lambda: clear(f_in))
    pl.when(y == 0)(lambda: clear(h_in))
    pl.when(z == nz - 1)(lambda: clear(zf_in))
    pl.when(z == 0)(lambda: clear(zh_in))
    odd = lax.rem(z, 2) == 1
    pl.when(odd)(lambda: clear(s_in))

    local[0].wait()
    swaps[0].wait_recv()
    total_heads = ldv.shape[1]
    pick = lax.broadcasted_iota(jnp.int32, (total_heads, heads), 0) == (
        lax.broadcasted_iota(jnp.int32, (total_heads, heads), 1) + core * heads
    )
    ld = dot(ldv[...], pick.astype(F32).astype(BF16), ((1,), (0,))).astype(BF16)
    at_row = lax.broadcasted_iota(jnp.int32, (both, both), 0)
    at_col = lax.broadcasted_iota(jnp.int32, (both, both), 1)
    lower = (at_row >= at_col).astype(F32).astype(BF16)
    chip_sum = dot(ld, jnp.ones((both, HEAD_DIM), BF16), ((0,), (0,)))
    zl[0] = chip_sum
    z_copies = [None] + [
        remote(zl.at[0], zl.at[k], zl_send.at[k], zl_recv.at[k], at_z(k)) for k in range(1, nz)
    ]
    for copy in z_copies[1:]:
        copy.start()
    cum = dot(lower, ld, ((1,), (0,)))
    cum_rows = dot(ld, lower, ((0,), (1,)))
    for i in range(heads):
        cum_b[i] = jnp.broadcast_to(cum[:, i : i + 1], (both, HEAD_DIM))
        cum_t[i] = jnp.broadcast_to(cum_rows[i : i + 1, :], (8, both))

    for j in (0, 1):
        local[1 + j].wait()
        swaps[1 + j].wait_recv()

    def columns(i):
        return pl.ds(pl.multiple_of(i * HEAD_DIM, HEAD_DIM), HEAD_DIM)

    def state_copy(kind, src, dst, p, to):
        return remote(src.at[p], dst.at[p], st_send.at[kind, p], st_recv.at[kind, p], to)

    def make_state(i, carry):
        scaled = qv[:, columns(i)].astype(F32) * jnp.exp(cum_b[i])
        high = scaled.astype(BF16)
        low = (scaled - high.astype(F32)).astype(BF16)
        g = gv[:, columns(i)]
        state = dot(high, g, ((0,), (0,))) + dot(low, g, ((0,), (0,)))
        for r in range(SPLIT):
            states[i * SPLIT + r] = state[r * rows : (r + 1) * rows]

        @pl.when(odd)
        def _():
            for r in range(SPLIT):
                state_copy(KS, states, s_in, i * SPLIT + r, at_z(-1)).start()

        return carry

    lax.fori_loop(0, heads, make_state, 0)

    before = jnp.zeros((heads, HEAD_DIM), F32)
    after = jnp.zeros((heads, HEAD_DIM), F32)
    for k in range(1, nz):
        z_copies[k].wait_recv()
        part = zl[k]
        before += jnp.where(k <= z, part, 0.0)
        after += jnp.where(k > z, part, 0.0)
    ps[0, 0] = before
    ps[0, 1] = after + chip_sum
    c_copies = [None] + [
        remote(ps.at[0], ps.at[k], ps_send.at[k], ps_recv.at[k], at_c(-k)) for k in range(1, ny + 1)
    ]
    for copy in c_copies[1:]:
        copy.start()
    for copy in c_copies[1:]:
        copy.wait_recv()

    def path(a, b):
        if a == b:
            return jnp.zeros((heads, HEAD_DIM), F32)
        total = ps[a, 1] + ps[b, 0]
        for m in range(a + 1, b):
            total = total + (ps[m, 0] + ps[m, 1])
        return total

    def by_y(choices):
        out = choices[0]
        for value in range(1, ny):
            out = jnp.where(y == value, choices[value], out)
        return out

    wt[WX] = jnp.exp(path(0, ny))
    wt[WY] = jnp.exp(path(0, 1))
    wt[WH] = jnp.exp(by_y([path(ny - v, ny) for v in range(ny)]))
    wt[WA] = jnp.exp(by_y([path(1, ny - v) for v in range(ny)]))
    wt[WZ] = jnp.exp(chip_sum)
    wt[WZH] = jnp.exp(ps[1, 0])
    wt[WU] = jnp.exp(after)

    local[3].wait()
    swaps[3].wait_recv()

    def weight(kind, p):
        return wt[kind, pl.ds(lax.div(p, SPLIT), 1), :]

    def link(kind, src, dst, to, has_in, has_out):
        def take(p):
            pl.when(has_in)(lambda: state_copy(kind, src, dst, p, to).wait_recv())

        def give(p):
            pl.when(has_out)(lambda: state_copy(kind, src, dst, p, to).start())

        def sent(p):
            pl.when(has_out)(lambda: state_copy(kind, src, dst, p, to).wait_send())

        return take, give, sent

    chain_c = link(KC, c_out, c_in, at_c(-ny), x < nx - 1, x > 0)
    chain_f = link(KF, f_out, f_in, at_c(-1), y < ny - 1, y > 0)
    chain_h = link(KH, h_out, h_in, at_c(1), y > 0, y < ny - 1)
    chain_zf = link(KZF, zf_out, zf_in, at_z(-1), z < nz - 1, z > 0)
    chain_zh = link(KZH, zh_out, zh_in, at_z(1), z > 0, z < nz - 1)
    chain_s = link(KS, states, s_in, at_z(-1), jnp.logical_not(odd), odd)
    own_share = (1 - lax.rem(z, 2)).astype(F32)

    def step_c(p):
        chain_c[0](p)
        c_out[p] = states[p] + weight(WX, p) * c_in[p]
        chain_c[1](p)

    def step_f(p):
        chain_f[0](p)
        f_out[p] = c_out[p] + weight(WY, p) * f_in[p]
        chain_f[1](p)

    def step_h(p):
        chain_h[0](p)
        h_out[p] = h_in[p] + weight(WH, p) * c_in[p]
        chain_h[1](p)

    def step_a(p):
        a_plus[p] = f_in[p] + weight(WA, p) * h_out[p]

    def step_zf(p):
        chain_s[0](p)
        chain_zf[0](p)
        zf_out[p] = (
            states[p] * own_share + weight(WY, p) * a_plus[p] + weight(WZ, p) * (zf_in[p] + s_in[p])
        )
        chain_zf[1](p)

    def step_zh(p):
        chain_zh[0](p)
        zh_out[p] = zh_in[p] + weight(WZH, p) * a_plus[p]
        chain_zh[1](p)

    def out_copies(i):
        place = columns(core * heads + i)
        here = pltpu.make_async_copy(out_v.at[i, mine], out_hbm.at[:, place], o_local.at[i])
        there = remote(out_v.at[i, other], out_hbm.at[:, place], o_send.at[i], o_recv.at[i], peer)
        return here, there

    def step_out(p):
        i = lax.div(p, SPLIT)

        @pl.when(lax.rem(p, SPLIT) == SPLIT - 1)
        def _():
            parts = []
            for r in range(SPLIT):
                at = i * SPLIT + r
                parts.append(zf_in[at] + s_in[at] * (1.0 / HEAD_DIM) + weight(WU, at) * zh_out[at])
            state = jnp.concatenate(parts, axis=0) if SPLIT > 1 else parts[0]
            high = state.astype(BF16)
            low = (state - high.astype(F32)).astype(BF16)
            keys = kv[:, columns(i)]
            carried = dot(keys, high, ((1,), (0,))) + dot(keys, low, ((1,), (0,)))
            logs = cum_b[i]
            to_end = jnp.exp(logs[both - 1 :, :] - logs)
            out_v[i] = (inside[i] + to_end * carried).astype(BF16)
            here, there = out_copies(i)
            here.start()
            there.start()

    def step_inside(p):
        i = lax.div(p, SPLIT)

        @pl.when(lax.rem(p, SPLIT) == 0)
        def _():
            scores = dot(kv[:, columns(i)], qv[:, columns(i)], ((1,), (1,))) * (1.0 / HEAD_DIM)
            start = cum_b[i]
            gaps = cum_t[i, 0:1, :] - jnp.concatenate([start] * (both // HEAD_DIM), axis=1)
            seen = lax.broadcasted_iota(jnp.int32, (both, both), 1) >= lax.broadcasted_iota(
                jnp.int32, (both, both), 0
            )
            table = jnp.where(seen, jnp.exp(jnp.where(seen, gaps, 0.0)), 0.0)
            inside[i] = dot((scores * table).astype(BF16), gv[:, columns(i)], ((1,), (0,)))

    far = jnp.maximum(z, nz - 1 - z)
    base_y = (nx - 1) * HOP
    base_z = base_y + (ny - 1) * HOP
    plan = (
        (step_c, (nx - 1 - x) * HOP),
        (step_f, base_y + (ny - 1 - y) * HOP),
        (step_h, base_y + y * HOP),
        (step_a, base_y + jnp.maximum(y, ny - 1 - y) * HOP),
        (step_zf, base_z + (nz - 1 - z) * HOP),
        (step_zh, base_z + z * HOP),
        (step_inside, 0),
        (step_out, base_z + far * HOP),
    )

    def step(t, carry):
        for act, delay in plan:
            p = t - delay

            @pl.when(jnp.logical_and(p >= 0, p < pieces))
            def _(act=act, p=p):
                act(p)

        return carry

    lax.fori_loop(0, base_z + far * HOP + pieces, step, 0)

    def finish(p, carry):
        for chain in (chain_c, chain_f, chain_h, chain_zf, chain_zh, chain_s):
            chain[2](p)
        return carry

    lax.fori_loop(0, pieces, finish, 0)

    def finish_out(i, carry):
        here, there = out_copies(i)
        here.wait()
        there.wait_send()
        there.wait_recv()
        return carry

    lax.fori_loop(0, heads, finish_out, 0)
    for copy in z_copies[1:] + c_copies[1:] + swaps:
        copy.wait_send()


def local(dims, queries, keys, out_grad, log_decay):
    nx, ny, nz, heads, tok = dims
    pieces = heads * SPLIT
    rows = HEAD_DIM // SPLIT
    cols = heads * HEAD_DIM
    both = 2 * tok

    def piece_buffer():
        return pltpu.VMEM((pieces, rows, HEAD_DIM), F32)

    dma = pltpu.SemaphoreType.DMA
    scratch = [pltpu.VMEM((both, cols), BF16)] * 3
    scratch += [
        pltpu.VMEM((both, 2 * heads), BF16),
        pltpu.VMEM((heads, both, HEAD_DIM), F32),
        pltpu.VMEM((heads, 8, both), F32),
        pltpu.VMEM((nz, heads, HEAD_DIM), F32),
        pltpu.VMEM((ny + 1, 2, heads, HEAD_DIM), F32),
        pltpu.VMEM((7, heads, HEAD_DIM), F32),
    ]
    scratch += [piece_buffer() for _ in range(13)]
    scratch += [
        pltpu.VMEM((heads, both, HEAD_DIM), F32),
        pltpu.VMEM((heads, both, HEAD_DIM), BF16),
        dma((4,)), dma((4,)), dma((4,)),
        dma((nz,)), dma((nz,)),
        dma((ny + 1,)), dma((ny + 1,)),
        dma((6, pieces)), dma((6, pieces)),
        dma((heads,)), dma((heads,)), dma((heads,)),
    ]
    any_space = pl.BlockSpec(memory_space=pl.ANY)
    return pl.pallas_call(
        functools.partial(kernel, dims),
        out_shape=jax.ShapeDtypeStruct(queries.shape, queries.dtype),
        in_specs=[any_space] * 4,
        out_specs=any_space,
        scratch_shapes=scratch,
        compiler_params=pltpu.CompilerParams(
            collective_id=0, has_side_effects=True, vmem_limit_bytes=48 * 1024 * 1024
        ),
    )(queries, keys, out_grad, log_decay)


def solution(mesh):
    groups, members = mesh.shape["ctx"], mesh.shape["sp"]
    ny = 1
    while ny * ny < groups:
        ny *= 2
    placed = P(("ctx", "sp"), None)

    def run(queries, keys, out_grad, log_decay):
        dims = (groups // ny, ny, members // 2, log_decay.shape[1] // 2, queries.shape[0])
        return local(dims, queries, keys, out_grad, log_decay)

    return jax.shard_map(run, mesh=mesh, in_specs=(placed,) * 4, out_specs=placed, check_vma=False)
```

```python
import functools

import jax
import jax.numpy as jnp
from jax import lax
from jax.experimental import pallas as pl
from jax.experimental.pallas import tpu as pltpu
from jax.sharding import PartitionSpec as P

HEAD_DIM = 128
HALF = HEAD_DIM // 2
MESH = pl.DeviceIdType.MESH
F32 = jnp.float32
BF16 = jnp.bfloat16
SUB = 2
HOP = 5
KEEP = 2
LAG = 6
EARLY = 4
VMEM_MIB = 62


def dot(a, b, contract):
    return lax.dot_general(a, b, (contract, ((), ())), preferred_element_type=F32)


def kernel(dims, *refs):
    nc, nz, heads, tok = dims
    (q_hbm, k_hbm, g_hbm, ld_hbm, out_hbm, qv, kv, gv, ldv, cum_b, cum_t, zl, w_out, w_in, s_out, s_in, a_buf, f_in, f_out,
     h_in, h_out, u_out, u_in, inside, out_v, in_local, in_send, in_recv, zl_send, zl_recv, w_send, w_recv, s_send,
     s_recv, f_send, f_recv, h_send, h_recv, u_send, u_recv, o_local, o_send, o_recv) = refs
    pairs = nz // 2
    rows = HALF // SUB
    cols = heads * HEAD_DIM
    both = 2 * tok
    c = lax.axis_index("ctx")
    s = lax.axis_index("sp")
    z, core = lax.div(s, 2), lax.rem(s, 2)
    pair, side = lax.div(z, 2), lax.rem(z, 2)
    peer = (c, z * 2 + 1 - core)

    def at_z(k):
        return (c, lax.rem(z + k + nz, nz) * 2 + core)

    def member(group, which):
        return (group, (pair * 2 + which) * 2 + core)

    def turned(k):
        return lax.rem(c + (1 - 2 * core) * k + nc, nc)

    mine = pl.ds(pl.multiple_of(core * tok, tok), tok)
    other = pl.ds(pl.multiple_of((1 - core) * tok, tok), tok)
    my_cols = pl.ds(pl.multiple_of(core * cols, cols), cols)
    peer_cols = pl.ds(pl.multiple_of((1 - core) * cols, cols), cols)

    ins = ((q_hbm, qv), (g_hbm, gv), (k_hbm, kv))
    local = [pltpu.make_async_copy(ld_hbm, ldv.at[:, mine], in_local.at[3])]
    for j, (src, dst) in enumerate(ins):
        local.append(pltpu.make_async_copy(src.at[:, my_cols], dst.at[mine], in_local.at[j]))
    for copy in local:
        copy.start()

    barrier = pltpu.get_barrier_semaphore()
    friends = []
    for k in range(nz // 2, 0, -1):
        friends += [at_z(k)] if 2 * k == nz else [at_z(k), at_z(-k)]
    for k in range(1, nc):
        friends += [member(lax.rem(c + k, nc), 0), member(lax.rem(c + k, nc), 1)]
    friends.append(peer)
    for friend in friends:
        pl.semaphore_signal(barrier, inc=1, device_id=friend, device_id_type=MESH)
    pl.semaphore_wait(barrier, len(friends))

    def remote(src, dst, send, recv, to):
        return pltpu.make_async_remote_copy(
            src_ref=src, dst_ref=dst, send_sem=send, recv_sem=recv, device_id=to, device_id_type=MESH
        )

    swaps = [remote(ld_hbm, ldv.at[:, mine], in_send.at[3], in_recv.at[3], peer)]
    for j, (src, dst) in enumerate(ins):
        swaps.append(remote(src.at[:, peer_cols], dst.at[mine], in_send.at[j], in_recv.at[j], peer))
    for copy in swaps:
        copy.start()

    def clear(ref):
        ref[...] = jnp.zeros(ref.shape, ref.dtype)

    last = pair == pairs - 1
    first = pair == 0
    pl.when(last)(lambda: clear(f_in))
    pl.when(first)(lambda: clear(h_in))
    a_buf[nc] = jnp.zeros((HALF, HEAD_DIM), F32)

    local[0].wait()
    swaps[0].wait_recv()
    total_heads = ldv.shape[0]
    pick = lax.broadcasted_iota(jnp.int32, (heads, total_heads), 1) == (
        lax.broadcasted_iota(jnp.int32, (heads, total_heads), 0) + core * heads
    )
    ld = dot(pick.astype(F32).astype(BF16), ldv[...], ((1,), (0,))).astype(BF16)
    at_row = lax.broadcasted_iota(jnp.int32, (both, both), 0)
    at_col = lax.broadcasted_iota(jnp.int32, (both, both), 1)
    lower = (at_row >= at_col).astype(F32).astype(BF16)
    chip_sum = dot(ld, jnp.ones((both, HEAD_DIM), BF16), ((1,), (0,)))
    zl[0] = chip_sum
    z_copies = [None] + [
        remote(zl.at[0], zl.at[k], zl_send.at[k], zl_recv.at[k], at_z(k)) for k in range(1, nz)
    ]
    for k in sorted(range(1, nz), key=lambda k: -min(k, nz - k)):
        z_copies[k].start()
    cum = dot(lower, ld, ((1,), (1,)))
    cum_rows = dot(ld, lower, ((1,), (1,)))
    for i in range(heads):
        cum_b[i] = jnp.broadcast_to(cum[:, i : i + 1], (both, HEAD_DIM))
        cum_t[i] = jnp.broadcast_to(cum_rows[i : i + 1, :], (8, both))

    def columns(i):
        return pl.ds(pl.multiple_of(i * HEAD_DIM, HEAD_DIM), HEAD_DIM)

    for j in (0, 1):
        local[1 + j].wait()
        swaps[1 + j].wait_recv()

    def half(r):
        return pl.ds(r * HALF, HALF)

    def part_of(sub, start=0):
        return pl.ds(pl.multiple_of(start + sub * rows, 8), rows)

    def s_copy(i, r, sub):
        return remote(
            s_out.at[i, part_of(sub, r * HALF)], s_in.at[c, side, part_of(sub)], s_send.at[i, r, sub],
            s_recv.at[c, side, sub], member(i, r),
        )

    def s_arrival(group, which, sub):
        there = s_in.at[group, which, part_of(sub)]
        return remote(there, there, s_send.at[group, which, sub], s_recv.at[group, which, sub], member(group, which))

    def w_copy(i, r):
        return remote(w_out.at[i], w_in.at[c, side], w_send.at[i, r], w_recv.at[c, side], member(i, r))

    def w_arrival(group, which):
        there = w_in.at[group, which]
        return remote(there, there, w_send.at[group, which], w_recv.at[group, which], member(group, which))

    def is_me(group, which):
        return jnp.logical_and(group == c, which == side)

    def not_me(group, which):
        return jnp.logical_or(group != c, which != side)

    def make_state(k, carry):
        i = turned(1 + k)
        scaled = qv[:, columns(i)].astype(F32) * jnp.exp(cum_b[i])
        high = scaled.astype(BF16)
        low = (scaled - high.astype(F32)).astype(BF16)
        g = gv[:, columns(i)]
        state = dot(high, g, ((0,), (0,))) + dot(low, g, ((0,), (0,)))
        s_out[i] = state
        for r in (0, 1):
            @pl.when(is_me(i, r))
            def _(r=r):
                s_in[c, side] = state[r * HALF : (r + 1) * HALF]

            @pl.when(not_me(i, r))
            def _(r=r):
                s_copy(i, r, 0).start()

        return carry

    lax.fori_loop(0, heads, make_state, 0)

    before = jnp.zeros((heads, HEAD_DIM), F32)
    after = jnp.zeros((heads, HEAD_DIM), F32)
    pair_sum = chip_sum
    for k in range(1, nz):
        z_copies[k].wait_recv()
        part = zl[k]
        at = lax.rem(z - k + nz, nz)
        before += jnp.where(at < pair * 2, part, 0.0)
        after += jnp.where(at > pair * 2 + 1, part, 0.0)
        pair_sum += jnp.where(lax.div(at, 2) == pair, part, 0.0)
    facts = (chip_sum, before, after + pair_sum, after)
    for i in range(heads):
        for n, fact in enumerate(facts):
            w_out[i, n : n + 1] = fact[i : i + 1]
        w_out[i, 4:8] = jnp.zeros((4, HEAD_DIM), F32)

    def give_weights(k, carry):
        i = turned(1 + k)
        for r in (0, 1):
            @pl.when(is_me(i, r))
            def _():
                w_in[c, side] = w_out[i]

            @pl.when(not_me(i, r))
            def _(r=r):
                w_copy(i, r).start()

        return carry

    lax.fori_loop(0, heads, give_weights, 0)

    for sub in range(1, SUB):
        def give_states(k, carry, sub=sub):
            i = turned(1 + k)
            for r in (0, 1):
                @pl.when(not_me(i, r))
                def _(r=r):
                    s_copy(i, r, sub).start()

            return carry

        lax.fori_loop(0, heads, give_states, 0)

    local[3].wait()
    swaps[3].wait_recv()

    def make_inside(i, carry):
        scores = dot(kv[:, columns(i)], qv[:, columns(i)], ((1,), (1,))) * (1.0 / HEAD_DIM)
        start = cum_b[i]
        gaps = cum_t[i, 0:1, :] - jnp.concatenate([start] * (both // HEAD_DIM), axis=1)
        seen = lax.broadcasted_iota(jnp.int32, (both, both), 1) >= lax.broadcasted_iota(
            jnp.int32, (both, both), 0
        )
        table = jnp.where(seen, jnp.exp(jnp.where(seen, gaps, 0.0)), 0.0)
        inside[i] = dot((scores * table).astype(BF16), gv[:, columns(i)], ((1,), (0,)))
        return carry

    lax.fori_loop(0, heads, make_inside, 0)

    def scan(sub):
        at = part_of(sub)

        def scan_group(k, carry):
            group = nc - 1 - k
            for which in (0, 1):
                @pl.when(not_me(group, which))
                def _(which=which):
                    if sub == 0:
                        w_arrival(group, which).wait_recv()
                    s_arrival(group, which, sub).wait_recv()

            behind = jnp.minimum(group + 1, nc - 1)
            to_next = jnp.exp(w_in[group, 0, 2:3] + w_in[behind, 0, 1:2])
            block = s_in[group, 0, at] + jnp.exp(w_in[group, 0, 0:1]) * s_in[group, 1, at]
            a_buf[group, at] = block + to_next * a_buf[group + 1, at]
            return carry

        lax.fori_loop(0, nc, scan_group, 0)

    scan(0)

    steps = nc * SUB

    def place(p):
        return turned(lax.rem(p, nc)), lax.div(p, nc)

    def spot(p):
        group, sub = place(p)
        return group * SUB + sub

    def f_copy(p):
        return remote(f_out.at[spot(p)], f_in.at[spot(p)], f_send.at[spot(p)], f_recv.at[spot(p)], at_z(-2))

    def h_copy(p):
        return remote(h_out.at[spot(p)], h_in.at[spot(p)], h_send.at[spot(p)], h_recv.at[spot(p)], at_z(2))

    def u_copy(group, which, sub):
        return remote(
            u_out.at[which, group, part_of(sub)], u_in.at[c, part_of(sub, side * HALF)],
            u_send.at[which, group, sub], u_recv.at[c, side, sub], member(group, which),
        )

    def u_arrival(i, r, sub):
        there = u_in.at[i, part_of(sub, r * HALF)]
        return remote(there, there, u_send.at[0, 0, 0], u_recv.at[i, r, sub], member(i, r))

    def step_f(p):
        group, sub = place(p)
        pl.when(jnp.logical_not(last))(lambda: f_copy(p).wait_recv())
        own = jnp.exp(w_in[group, 0, 0:1] + w_in[group, 1, 0:1])
        f_out[spot(p)] = a_buf[group, part_of(sub)] + own * f_in[spot(p)]

        @pl.when(jnp.logical_not(first))
        def _():
            pl.when(p >= KEEP)(lambda: f_copy(p - KEEP).wait_send())
            f_copy(p).start()

    def step_h(p):
        group, sub = place(p)
        pl.when(jnp.logical_not(first))(lambda: h_copy(p).wait_recv())
        behind = jnp.minimum(group + 1, nc - 1)
        h_out[spot(p)] = h_in[spot(p)] + jnp.exp(w_in[behind, 0, 1:2]) * a_buf[group + 1, part_of(sub)]

        @pl.when(jnp.logical_not(last))
        def _():
            pl.when(p >= KEEP)(lambda: h_copy(p - KEEP).wait_send())
            h_copy(p).start()

    def step_u(p):
        group, sub = place(p)
        state = f_in[spot(p)] + jnp.exp(w_in[group, 0, 3:4]) * h_out[spot(p)]
        u_out[1, group, part_of(sub)] = state
        u_out[0, group, part_of(sub)] = (
            s_in[group, 1, part_of(sub)] * (1.0 / HEAD_DIM) + jnp.exp(w_in[group, 1, 0:1]) * state
        )

        for which in (0, 1):
            @pl.when(is_me(group, which))
            def _(which=which):
                u_in[c, part_of(sub, side * HALF)] = u_out[which, group, part_of(sub)]

            @pl.when(not_me(group, which))
            def _(which=which):
                u_copy(group, which, sub).start()

    def out_copies(i):
        at = columns(core * heads + i)
        here = pltpu.make_async_copy(out_v.at[i, mine], out_hbm.at[:, at], o_local.at[i])
        there = remote(out_v.at[i, other], out_hbm.at[:, at], o_send.at[i], o_recv.at[i], peer)
        return here, there

    def step_out(p):
        i = turned(-lax.rem(p, nc))

        @pl.when(p >= nc * (SUB - 1))
        def _():
            for r in (0, 1):
                @pl.when(not_me(i, r))
                def _(r=r):
                    for sub in range(SUB):
                        u_arrival(i, r, sub).wait_recv()

            state = u_in[i]
            high = state.astype(BF16)
            low = (state - high.astype(F32)).astype(BF16)
            keys = kv[:, columns(i)]
            carried = dot(keys, high, ((1,), (0,))) + dot(keys, low, ((1,), (0,)))
            logs = cum_b[i]
            to_end = jnp.exp(logs[both - 1 :, :] - logs)
            out_v[i] = (inside[i] + to_end * carried).astype(BF16)
            here, there = out_copies(i)
            here.start()
            there.start()

    far = jnp.maximum(pair, pairs - 1 - pair) * HOP
    plan = (
        (step_f, (pairs - 1 - pair) * HOP),
        (step_h, pair * HOP),
        (step_u, far),
        (step_out, far + LAG),
    )

    def step(t, carry):
        for sub in range(1, SUB):
            pl.when(t == sub * nc - EARLY)(functools.partial(scan, sub))
        for act, delay in plan:
            p = t - delay

            @pl.when(jnp.logical_and(p >= 0, p < steps))
            def _(act=act, p=p):
                act(p)

        return carry

    lax.fori_loop(0, far + LAG + steps, step, 0)

    def finish_chain(p, carry):
        pl.when(jnp.logical_not(first))(lambda: f_copy(p).wait_send())
        pl.when(jnp.logical_not(last))(lambda: h_copy(p).wait_send())
        return carry

    lax.fori_loop(steps - KEEP, steps, finish_chain, 0)

    def finish(i, carry):
        for r in (0, 1):
            @pl.when(not_me(i, r))
            def _(r=r):
                w_copy(i, r).wait_send()
                for sub in range(SUB):
                    s_copy(i, r, sub).wait_send()
                    u_copy(i, r, sub).wait_send()

        here, there = out_copies(i)
        here.wait()
        there.wait_send()
        there.wait_recv()
        return carry

    lax.fori_loop(0, heads, finish, 0)
    for copy in z_copies[1:] + swaps:
        copy.wait_send()


def local(dims, queries, keys, out_grad, log_decay):
    nc, nz, heads, tok = dims
    cols = heads * HEAD_DIM
    both = 2 * tok
    rows = HALF // SUB
    dma = pltpu.SemaphoreType.DMA

    def floats(*shape):
        return pltpu.VMEM(shape, F32)

    scratch = [pltpu.VMEM((both, cols), BF16)] * 3
    scratch += [
        pltpu.VMEM((2 * heads, both), BF16),
        floats(heads, both, HEAD_DIM),
        floats(heads, 8, both),
        floats(nz, heads, HEAD_DIM),
        floats(heads, 8, HEAD_DIM),
        floats(nc, 2, 8, HEAD_DIM),
        floats(heads, HEAD_DIM, HEAD_DIM),
        floats(nc, 2, HALF, HEAD_DIM),
        floats(nc + 1, HALF, HEAD_DIM),
    ]
    scratch += [floats(nc * SUB, rows, HEAD_DIM) for _ in range(4)]
    scratch += [
        floats(2, nc, HALF, HEAD_DIM),
        floats(heads, HEAD_DIM, HEAD_DIM),
        floats(heads, both, HEAD_DIM),
        pltpu.VMEM((heads, both, HEAD_DIM), BF16),
        dma((4,)), dma((4,)), dma((4,)),
        dma((nz,)), dma((nz,)),
        dma((heads, 2)), dma((nc, 2)),
        dma((heads, 2, SUB)), dma((nc, 2, SUB)),
        dma((nc * SUB,)), dma((nc * SUB,)),
        dma((nc * SUB,)), dma((nc * SUB,)),
        dma((2, nc, SUB)), dma((heads, 2, SUB)),
        dma((heads,)), dma((heads,)), dma((heads,)),
    ]
    far = pl.BlockSpec(memory_space=pltpu.HBM)
    return pl.pallas_call(
        functools.partial(kernel, dims),
        out_shape=jax.ShapeDtypeStruct(queries.shape, queries.dtype),
        in_specs=[far] * 4,
        out_specs=far,
        scratch_shapes=scratch,
        compiler_params=pltpu.CompilerParams(
            collective_id=0, has_side_effects=True, vmem_limit_bytes=VMEM_MIB * 1024 * 1024
        ),
    )(queries, keys, out_grad, log_decay.T)


def solution(mesh):
    groups, members = mesh.shape["ctx"], mesh.shape["sp"]
    placed = P(("ctx", "sp"), None)

    def run(queries, keys, out_grad, log_decay):
        dims = (groups, members // 2, log_decay.shape[1] // 2, queries.shape[0])
        return local(dims, queries, keys, out_grad, log_decay)

    return jax.shard_map(run, mesh=mesh, in_specs=(placed,) * 4, out_specs=placed, check_vma=False)
```

```python
import functools

import jax
import jax.numpy as jnp
from jax import lax
from jax.experimental import pallas as pl
from jax.experimental.pallas import tpu as pltpu
from jax.sharding import PartitionSpec as P

HEAD_DIM = 128
HALF = HEAD_DIM // 2
MESH = pl.DeviceIdType.MESH
F32 = jnp.float32
BF16 = jnp.bfloat16
SUB = 2
HOP = 4
KEEP = 2
LAG = 6
EARLY = 4
VMEM_MIB = 62


def dot(a, b, contract):
    return lax.dot_general(a, b, (contract, ((), ())), preferred_element_type=F32)


def kernel(dims, *refs):
    nc, nz, heads, tok = dims
    (q_hbm, k_hbm, g_hbm, ld_hbm, out_hbm, qv, kv, gv, ldv, cum_b, cum_t, zl, w_out, w_in, s_out, s_in, a_buf, f_in, f_out,
     h_in, h_out, u_out, u_in, inside, out_v, in_local, in_send, in_recv, zl_send, zl_recv, w_send, w_recv, s_send,
     s_recv, f_send, f_recv, h_send, h_recv, u_send, u_recv, o_local, o_send, o_recv) = refs
    pairs = nz // 2
    rows = HALF // SUB
    cols = heads * HEAD_DIM
    both = 2 * tok
    c = lax.axis_index("ctx")
    s = lax.axis_index("sp")
    z, core = lax.div(s, 2), lax.rem(s, 2)
    pair, side = lax.div(z, 2), lax.rem(z, 2)
    peer = (c, z * 2 + 1 - core)

    def at_z(k):
        return (c, lax.rem(z + k + nz, nz) * 2 + core)

    def member(group, which):
        return (group, (pair * 2 + which) * 2 + core)

    def turned(k):
        return lax.rem(c + (1 - 2 * core) * k + nc, nc)

    mine = pl.ds(pl.multiple_of(core * tok, tok), tok)
    other = pl.ds(pl.multiple_of((1 - core) * tok, tok), tok)
    my_cols = pl.ds(pl.multiple_of(core * cols, cols), cols)
    peer_cols = pl.ds(pl.multiple_of((1 - core) * cols, cols), cols)

    ins = ((q_hbm, qv), (g_hbm, gv), (k_hbm, kv))
    local = [pltpu.make_async_copy(ld_hbm, ldv.at[:, mine], in_local.at[3])]
    for j, (src, dst) in enumerate(ins):
        local.append(pltpu.make_async_copy(src.at[:, my_cols], dst.at[mine], in_local.at[j]))
    for copy in local:
        copy.start()

    barrier = pltpu.get_barrier_semaphore()
    friends = []
    for k in range(nz // 2, 0, -1):
        friends += [at_z(k)] if 2 * k == nz else [at_z(k), at_z(-k)]
    for k in range(1, nc):
        friends += [member(lax.rem(c + k, nc), 0), member(lax.rem(c + k, nc), 1)]
    friends.append(peer)
    for friend in friends:
        pl.semaphore_signal(barrier, inc=1, device_id=friend, device_id_type=MESH)
    pl.semaphore_wait(barrier, len(friends))

    def remote(src, dst, send, recv, to):
        return pltpu.make_async_remote_copy(
            src_ref=src, dst_ref=dst, send_sem=send, recv_sem=recv, device_id=to, device_id_type=MESH
        )

    swaps = [remote(ld_hbm, ldv.at[:, mine], in_send.at[3], in_recv.at[3], peer)]
    for j, (src, dst) in enumerate(ins):
        swaps.append(remote(src.at[:, peer_cols], dst.at[mine], in_send.at[j], in_recv.at[j], peer))
    for copy in swaps:
        copy.start()

    def clear(ref):
        ref[...] = jnp.zeros(ref.shape, ref.dtype)

    last = pair == pairs - 1
    first = pair == 0
    pl.when(last)(lambda: clear(f_in))
    pl.when(first)(lambda: clear(h_in))
    a_buf[nc] = jnp.zeros((HALF, HEAD_DIM), F32)

    local[0].wait()
    swaps[0].wait_recv()
    total_heads = ldv.shape[0]
    pick = lax.broadcasted_iota(jnp.int32, (heads, total_heads), 1) == (
        lax.broadcasted_iota(jnp.int32, (heads, total_heads), 0) + core * heads
    )
    ld = dot(pick.astype(F32).astype(BF16), ldv[...], ((1,), (0,))).astype(BF16)
    at_row = lax.broadcasted_iota(jnp.int32, (both, both), 0)
    at_col = lax.broadcasted_iota(jnp.int32, (both, both), 1)
    lower = (at_row >= at_col).astype(F32).astype(BF16)
    chip_sum = dot(ld, jnp.ones((both, HEAD_DIM), BF16), ((1,), (0,)))
    zl[0] = chip_sum
    z_copies = [None] + [
        remote(zl.at[0], zl.at[k], zl_send.at[k], zl_recv.at[k], at_z(k)) for k in range(1, nz)
    ]
    for k in sorted(range(1, nz), key=lambda k: -min(k, nz - k)):
        z_copies[k].start()
    cum = dot(lower, ld, ((1,), (1,)))
    cum_rows = dot(ld, lower, ((1,), (1,)))
    for i in range(heads):
        cum_b[i] = jnp.broadcast_to(cum[:, i : i + 1], (both, HEAD_DIM))
        cum_t[i] = jnp.broadcast_to(cum_rows[i : i + 1, :], (8, both))

    def columns(i):
        return pl.ds(pl.multiple_of(i * HEAD_DIM, HEAD_DIM), HEAD_DIM)

    for j in (0, 1):
        local[1 + j].wait()
        swaps[1 + j].wait_recv()

    def half(r):
        return pl.ds(r * HALF, HALF)

    def part_of(sub, start=0):
        return pl.ds(pl.multiple_of(start + sub * rows, 8), rows)

    def s_copy(i, r, sub):
        return remote(
            s_out.at[i, part_of(sub, r * HALF)], s_in.at[c, side, part_of(sub)], s_send.at[i, r, sub],
            s_recv.at[c, side, sub], member(i, r),
        )

    def s_arrival(group, which, sub):
        there = s_in.at[group, which, part_of(sub)]
        return remote(there, there, s_send.at[group, which, sub], s_recv.at[group, which, sub], member(group, which))

    def w_copy(i, r):
        return remote(w_out.at[i], w_in.at[c, side], w_send.at[i, r], w_recv.at[c, side], member(i, r))

    def w_arrival(group, which):
        there = w_in.at[group, which]
        return remote(there, there, w_send.at[group, which], w_recv.at[group, which], member(group, which))

    def is_me(group, which):
        return jnp.logical_and(group == c, which == side)

    def not_me(group, which):
        return jnp.logical_or(group != c, which != side)

    def make_state(k, carry):
        i = turned(1 + k)
        scaled = qv[:, columns(i)].astype(F32) * jnp.exp(cum_b[i])
        high = scaled.astype(BF16)
        low = (scaled - high.astype(F32)).astype(BF16)
        g = gv[:, columns(i)]
        state = dot(high, g, ((0,), (0,))) + dot(low, g, ((0,), (0,)))
        s_out[i] = state
        for r in (0, 1):
            @pl.when(is_me(i, r))
            def _(r=r):
                s_in[c, side] = state[r * HALF : (r + 1) * HALF]

            @pl.when(not_me(i, r))
            def _(r=r):
                s_copy(i, r, 0).start()

        return carry

    lax.fori_loop(0, heads, make_state, 0)

    before = jnp.zeros((heads, HEAD_DIM), F32)
    after = jnp.zeros((heads, HEAD_DIM), F32)
    pair_sum = chip_sum
    for k in range(1, nz):
        z_copies[k].wait_recv()
        part = zl[k]
        at = lax.rem(z - k + nz, nz)
        before += jnp.where(at < pair * 2, part, 0.0)
        after += jnp.where(at > pair * 2 + 1, part, 0.0)
        pair_sum += jnp.where(lax.div(at, 2) == pair, part, 0.0)
    facts = (chip_sum, before, after + pair_sum, after)
    for i in range(heads):
        for n, fact in enumerate(facts):
            w_out[i, n : n + 1] = fact[i : i + 1]
        w_out[i, 4:8] = jnp.zeros((4, HEAD_DIM), F32)

    def give_weights(k, carry):
        i = turned(1 + k)
        for r in (0, 1):
            @pl.when(is_me(i, r))
            def _():
                w_in[c, side] = w_out[i]

            @pl.when(not_me(i, r))
            def _(r=r):
                w_copy(i, r).start()

        return carry

    lax.fori_loop(0, heads, give_weights, 0)

    for sub in range(1, SUB):
        def give_states(k, carry, sub=sub):
            i = turned(1 + k)
            for r in (0, 1):
                @pl.when(not_me(i, r))
                def _(r=r):
                    s_copy(i, r, sub).start()

            return carry

        lax.fori_loop(0, heads, give_states, 0)

    local[3].wait()
    swaps[3].wait_recv()

    def make_inside(i, carry):
        scores = dot(kv[:, columns(i)], qv[:, columns(i)], ((1,), (1,))) * (1.0 / HEAD_DIM)
        start = cum_b[i]
        gaps = cum_t[i, 0:1, :] - jnp.concatenate([start] * (both // HEAD_DIM), axis=1)
        seen = lax.broadcasted_iota(jnp.int32, (both, both), 1) >= lax.broadcasted_iota(
            jnp.int32, (both, both), 0
        )
        table = jnp.where(seen, jnp.exp(jnp.where(seen, gaps, 0.0)), 0.0)
        inside[i] = dot((scores * table).astype(BF16), gv[:, columns(i)], ((1,), (0,)))
        return carry

    lax.fori_loop(0, heads, make_inside, 0)

    def scan(sub):
        at = part_of(sub)

        def scan_group(k, carry):
            group = nc - 1 - k
            for which in (0, 1):
                @pl.when(not_me(group, which))
                def _(which=which):
                    if sub == 0:
                        w_arrival(group, which).wait_recv()
                    s_arrival(group, which, sub).wait_recv()

            behind = jnp.minimum(group + 1, nc - 1)
            to_next = jnp.exp(w_in[group, 0, 2:3] + w_in[behind, 0, 1:2])
            block = s_in[group, 0, at] + jnp.exp(w_in[group, 0, 0:1]) * s_in[group, 1, at]
            a_buf[group, at] = block + to_next * a_buf[group + 1, at]
            return carry

        lax.fori_loop(0, nc, scan_group, 0)

    scan(0)

    steps = nc * SUB

    def place(p):
        return turned(lax.rem(p, nc)), lax.div(p, nc)

    def spot(p):
        group, sub = place(p)
        return group * SUB + sub

    def f_copy(p):
        return remote(f_out.at[spot(p)], f_in.at[spot(p)], f_send.at[spot(p)], f_recv.at[spot(p)], at_z(-2))

    def h_copy(p):
        return remote(h_out.at[spot(p)], h_in.at[spot(p)], h_send.at[spot(p)], h_recv.at[spot(p)], at_z(2))

    def u_copy(group, which, sub):
        return remote(
            u_out.at[which, group, part_of(sub)], u_in.at[c, part_of(sub, side * HALF)],
            u_send.at[which, group, sub], u_recv.at[c, side, sub], member(group, which),
        )

    def u_arrival(i, r, sub):
        there = u_in.at[i, part_of(sub, r * HALF)]
        return remote(there, there, u_send.at[0, 0, 0], u_recv.at[i, r, sub], member(i, r))

    def step_f(p):
        group, sub = place(p)
        pl.when(jnp.logical_not(last))(lambda: f_copy(p).wait_recv())
        own = jnp.exp(w_in[group, 0, 0:1] + w_in[group, 1, 0:1])
        f_out[spot(p)] = a_buf[group, part_of(sub)] + own * f_in[spot(p)]

        @pl.when(jnp.logical_not(first))
        def _():
            pl.when(p >= KEEP)(lambda: f_copy(p - KEEP).wait_send())
            f_copy(p).start()

    def step_h(p):
        group, sub = place(p)
        pl.when(jnp.logical_not(first))(lambda: h_copy(p).wait_recv())
        behind = jnp.minimum(group + 1, nc - 1)
        h_out[spot(p)] = h_in[spot(p)] + jnp.exp(w_in[behind, 0, 1:2]) * a_buf[group + 1, part_of(sub)]

        @pl.when(jnp.logical_not(last))
        def _():
            pl.when(p >= KEEP)(lambda: h_copy(p - KEEP).wait_send())
            h_copy(p).start()

    def step_u(p):
        group, sub = place(p)
        state = f_in[spot(p)] + jnp.exp(w_in[group, 0, 3:4]) * h_out[spot(p)]
        u_out[1, group, part_of(sub)] = state
        u_out[0, group, part_of(sub)] = (
            s_in[group, 1, part_of(sub)] * (1.0 / HEAD_DIM) + jnp.exp(w_in[group, 1, 0:1]) * state
        )

        for which in (0, 1):
            @pl.when(is_me(group, which))
            def _(which=which):
                u_in[c, part_of(sub, side * HALF)] = u_out[which, group, part_of(sub)]

            @pl.when(not_me(group, which))
            def _(which=which):
                u_copy(group, which, sub).start()

    def out_copies(i):
        at = columns(core * heads + i)
        here = pltpu.make_async_copy(out_v.at[i, mine], out_hbm.at[:, at], o_local.at[i])
        there = remote(out_v.at[i, other], out_hbm.at[:, at], o_send.at[i], o_recv.at[i], peer)
        return here, there

    def step_out(p):
        i = turned(-lax.rem(p, nc))

        @pl.when(p >= nc * (SUB - 1))
        def _():
            for r in (0, 1):
                @pl.when(not_me(i, r))
                def _(r=r):
                    for sub in range(SUB):
                        u_arrival(i, r, sub).wait_recv()

            state = u_in[i]
            high = state.astype(BF16)
            low = (state - high.astype(F32)).astype(BF16)
            keys = kv[:, columns(i)]
            carried = dot(keys, high, ((1,), (0,))) + dot(keys, low, ((1,), (0,)))
            logs = cum_b[i]
            to_end = jnp.exp(logs[both - 1 :, :] - logs)
            out_v[i] = (inside[i] + to_end * carried).astype(BF16)
            here, there = out_copies(i)
            here.start()
            there.start()

    far = jnp.maximum(pair, pairs - 1 - pair) * HOP
    plan = (
        (step_f, (pairs - 1 - pair) * HOP),
        (step_h, pair * HOP),
        (step_u, far),
        (step_out, far + LAG),
    )

    def step(t, carry):
        for sub in range(1, SUB):
            pl.when(t == sub * nc - EARLY)(functools.partial(scan, sub))
        for act, delay in plan:
            p = t - delay

            @pl.when(jnp.logical_and(p >= 0, p < steps))
            def _(act=act, p=p):
                act(p)

        return carry

    lax.fori_loop(0, far + LAG + steps, step, 0)

    def finish_chain(p, carry):
        pl.when(jnp.logical_not(first))(lambda: f_copy(p).wait_send())
        pl.when(jnp.logical_not(last))(lambda: h_copy(p).wait_send())
        return carry

    lax.fori_loop(steps - KEEP, steps, finish_chain, 0)

    def finish(i, carry):
        for r in (0, 1):
            @pl.when(not_me(i, r))
            def _(r=r):
                w_copy(i, r).wait_send()
                for sub in range(SUB):
                    s_copy(i, r, sub).wait_send()
                    u_copy(i, r, sub).wait_send()

        here, there = out_copies(i)
        here.wait()
        there.wait_send()
        there.wait_recv()
        return carry

    lax.fori_loop(0, heads, finish, 0)
    for copy in z_copies[1:] + swaps:
        copy.wait_send()


def local(dims, queries, keys, out_grad, log_decay):
    nc, nz, heads, tok = dims
    cols = heads * HEAD_DIM
    both = 2 * tok
    rows = HALF // SUB
    dma = pltpu.SemaphoreType.DMA

    def floats(*shape):
        return pltpu.VMEM(shape, F32)

    scratch = [pltpu.VMEM((both, cols), BF16)] * 3
    scratch += [
        pltpu.VMEM((2 * heads, both), BF16),
        floats(heads, both, HEAD_DIM),
        floats(heads, 8, both),
        floats(nz, heads, HEAD_DIM),
        floats(heads, 8, HEAD_DIM),
        floats(nc, 2, 8, HEAD_DIM),
        floats(heads, HEAD_DIM, HEAD_DIM),
        floats(nc, 2, HALF, HEAD_DIM),
        floats(nc + 1, HALF, HEAD_DIM),
    ]
    scratch += [floats(nc * SUB, rows, HEAD_DIM) for _ in range(4)]
    scratch += [
        floats(2, nc, HALF, HEAD_DIM),
        floats(heads, HEAD_DIM, HEAD_DIM),
        floats(heads, both, HEAD_DIM),
        pltpu.VMEM((heads, both, HEAD_DIM), BF16),
        dma((4,)), dma((4,)), dma((4,)),
        dma((nz,)), dma((nz,)),
        dma((heads, 2)), dma((nc, 2)),
        dma((heads, 2, SUB)), dma((nc, 2, SUB)),
        dma((nc * SUB,)), dma((nc * SUB,)),
        dma((nc * SUB,)), dma((nc * SUB,)),
        dma((2, nc, SUB)), dma((heads, 2, SUB)),
        dma((heads,)), dma((heads,)), dma((heads,)),
    ]
    far = pl.BlockSpec(memory_space=pltpu.HBM)
    return pl.pallas_call(
        functools.partial(kernel, dims),
        out_shape=jax.ShapeDtypeStruct(queries.shape, queries.dtype),
        in_specs=[far] * 4,
        out_specs=far,
        scratch_shapes=scratch,
        compiler_params=pltpu.CompilerParams(
            collective_id=0, has_side_effects=True, vmem_limit_bytes=VMEM_MIB * 1024 * 1024
        ),
    )(queries, keys, out_grad, log_decay.T)


def solution(mesh):
    groups, members = mesh.shape["ctx"], mesh.shape["sp"]
    placed = P(("ctx", "sp"), None)

    def run(queries, keys, out_grad, log_decay):
        dims = (groups, members // 2, log_decay.shape[1] // 2, queries.shape[0])
        return local(dims, queries, keys, out_grad, log_decay)

    return jax.shard_map(run, mesh=mesh, in_specs=(placed,) * 4, out_specs=placed, check_vma=False)
```

```python
import functools

import jax
import jax.numpy as jnp
from jax import lax
from jax.experimental import pallas as pl
from jax.experimental.pallas import tpu as pltpu
from jax.sharding import PartitionSpec as P

HEAD_DIM = 128
HALF = HEAD_DIM // 2
MESH = pl.DeviceIdType.MESH
F32 = jnp.float32
BF16 = jnp.bfloat16
SUB = 2
HOP = 4
KEEP = 2
LAG = 6
EARLY = 4
VMEM_MIB = 62


def dot(a, b, contract):
    return lax.dot_general(a, b, (contract, ((), ())), preferred_element_type=F32)


def kernel(dims, *refs):
    nc, nz, heads, tok = dims
    (q_hbm, k_hbm, g_hbm, ld_hbm, out_hbm, qv, kv, gv, ldv, cum_b, cum_t, zl, w_out, w_in, s_out, s_in, a_buf, f_in, f_out,
     h_in, h_out, u_out, u_in, inside, out_v, in_local, in_send, in_recv, zl_send, zl_recv, w_send, w_recv, s_send,
     s_recv, f_send, f_recv, h_send, h_recv, u_send, u_recv, o_local, o_send, o_recv) = refs
    pairs = nz // 2
    rows = HALF // SUB
    cols = heads * HEAD_DIM
    both = 2 * tok
    c = lax.axis_index("ctx")
    s = lax.axis_index("sp")
    z, core = lax.div(s, 2), lax.rem(s, 2)
    pair, side = lax.div(z, 2), lax.rem(z, 2)
    peer = (c, z * 2 + 1 - core)

    def at_z(k):
        return (c, lax.rem(z + k + nz, nz) * 2 + core)

    def member(group, which):
        return (group, (pair * 2 + which) * 2 + core)

    def turned(k):
        return lax.rem(c + (1 - 2 * core) * k + nc, nc)

    mine = pl.ds(pl.multiple_of(core * tok, tok), tok)
    other = pl.ds(pl.multiple_of((1 - core) * tok, tok), tok)
    my_cols = pl.ds(pl.multiple_of(core * cols, cols), cols)
    peer_cols = pl.ds(pl.multiple_of((1 - core) * cols, cols), cols)

    ins = ((q_hbm, qv), (g_hbm, gv), (k_hbm, kv))
    local = [pltpu.make_async_copy(ld_hbm, ldv.at[:, mine], in_local.at[3])]
    for j, (src, dst) in enumerate(ins):
        local.append(pltpu.make_async_copy(src.at[:, my_cols], dst.at[mine], in_local.at[j]))
    for copy in local:
        copy.start()

    barrier = pltpu.get_barrier_semaphore()
    friends = []
    for k in range(nz // 2, 0, -1):
        friends += [at_z(k)] if 2 * k == nz else [at_z(k), at_z(-k)]
    for k in range(1, nc):
        friends += [member(lax.rem(c + k, nc), 0), member(lax.rem(c + k, nc), 1)]
    friends.append(peer)
    for friend in friends:
        pl.semaphore_signal(barrier, inc=1, device_id=friend, device_id_type=MESH)
    pl.semaphore_wait(barrier, len(friends))

    def remote(src, dst, send, recv, to):
        return pltpu.make_async_remote_copy(
            src_ref=src, dst_ref=dst, send_sem=send, recv_sem=recv, device_id=to, device_id_type=MESH
        )

    swaps = [remote(ld_hbm, ldv.at[:, mine], in_send.at[3], in_recv.at[3], peer)]
    for j, (src, dst) in enumerate(ins):
        swaps.append(remote(src.at[:, peer_cols], dst.at[mine], in_send.at[j], in_recv.at[j], peer))
    for copy in swaps[:3]:
        copy.start()

    def clear(ref):
        ref[...] = jnp.zeros(ref.shape, ref.dtype)

    last = pair == pairs - 1
    first = pair == 0
    pl.when(last)(lambda: clear(f_in))
    pl.when(first)(lambda: clear(h_in))
    a_buf[nc] = jnp.zeros((HALF, HEAD_DIM), F32)

    local[0].wait()
    swaps[0].wait_recv()
    total_heads = ldv.shape[0]
    pick = lax.broadcasted_iota(jnp.int32, (heads, total_heads), 1) == (
        lax.broadcasted_iota(jnp.int32, (heads, total_heads), 0) + core * heads
    )
    ld = dot(pick.astype(F32).astype(BF16), ldv[...], ((1,), (0,))).astype(BF16)
    at_row = lax.broadcasted_iota(jnp.int32, (both, both), 0)
    at_col = lax.broadcasted_iota(jnp.int32, (both, both), 1)
    lower = (at_row >= at_col).astype(F32).astype(BF16)
    chip_sum = dot(ld, jnp.ones((both, HEAD_DIM), BF16), ((1,), (0,)))
    zl[0] = chip_sum
    z_copies = [None] + [
        remote(zl.at[0], zl.at[k], zl_send.at[k], zl_recv.at[k], at_z(k)) for k in range(1, nz)
    ]
    for k in sorted(range(1, nz), key=lambda k: -min(k, nz - k)):
        z_copies[k].start()
    cum = dot(lower, ld, ((1,), (1,)))
    cum_rows = dot(ld, lower, ((1,), (1,)))
    for i in range(heads):
        cum_b[i] = jnp.broadcast_to(cum[:, i : i + 1], (both, HEAD_DIM))
        cum_t[i] = jnp.broadcast_to(cum_rows[i : i + 1, :], (8, both))

    def columns(i):
        return pl.ds(pl.multiple_of(i * HEAD_DIM, HEAD_DIM), HEAD_DIM)

    for j in (0, 1):
        local[1 + j].wait()
        swaps[1 + j].wait_recv()

    def half(r):
        return pl.ds(r * HALF, HALF)

    def part_of(sub, start=0):
        return pl.ds(pl.multiple_of(start + sub * rows, 8), rows)

    def s_copy(i, r, sub):
        return remote(
            s_out.at[i, part_of(sub, r * HALF)], s_in.at[c, side, part_of(sub)], s_send.at[i, r, sub],
            s_recv.at[c, side, sub], member(i, r),
        )

    def s_arrival(group, which, sub):
        there = s_in.at[group, which, part_of(sub)]
        return remote(there, there, s_send.at[group, which, sub], s_recv.at[group, which, sub], member(group, which))

    def w_copy(i, r):
        return remote(w_out.at[i], w_in.at[c, side], w_send.at[i, r], w_recv.at[c, side], member(i, r))

    def w_arrival(group, which):
        there = w_in.at[group, which]
        return remote(there, there, w_send.at[group, which], w_recv.at[group, which], member(group, which))

    def is_me(group, which):
        return jnp.logical_and(group == c, which == side)

    def not_me(group, which):
        return jnp.logical_or(group != c, which != side)

    def make_state(k, carry):
        i = turned(1 + k)
        scaled = qv[:, columns(i)].astype(F32) * jnp.exp(cum_b[i])
        high = scaled.astype(BF16)
        low = (scaled - high.astype(F32)).astype(BF16)
        g = gv[:, columns(i)]
        state = dot(high, g, ((0,), (0,))) + dot(low, g, ((0,), (0,)))
        s_out[i] = state
        for r in (0, 1):
            @pl.when(is_me(i, r))
            def _(r=r):
                s_in[c, side] = state[r * HALF : (r + 1) * HALF]

            @pl.when(not_me(i, r))
            def _(r=r):
                s_copy(i, r, 0).start()

        return carry

    lax.fori_loop(0, heads, make_state, 0)
    swaps[3].start()

    before = jnp.zeros((heads, HEAD_DIM), F32)
    after = jnp.zeros((heads, HEAD_DIM), F32)
    pair_sum = chip_sum
    for k in range(1, nz):
        z_copies[k].wait_recv()
        part = zl[k]
        at = lax.rem(z - k + nz, nz)
        before += jnp.where(at < pair * 2, part, 0.0)
        after += jnp.where(at > pair * 2 + 1, part, 0.0)
        pair_sum += jnp.where(lax.div(at, 2) == pair, part, 0.0)
    facts = (chip_sum, before, after + pair_sum, after)
    for i in range(heads):
        for n, fact in enumerate(facts):
            w_out[i, n : n + 1] = fact[i : i + 1]
        w_out[i, 4:8] = jnp.zeros((4, HEAD_DIM), F32)

    def give_weights(k, carry):
        i = turned(1 + k)
        for r in (0, 1):
            @pl.when(is_me(i, r))
            def _():
                w_in[c, side] = w_out[i]

            @pl.when(not_me(i, r))
            def _(r=r):
                w_copy(i, r).start()

        return carry

    lax.fori_loop(0, heads, give_weights, 0)

    for sub in range(1, SUB):
        def give_states(k, carry, sub=sub):
            i = turned(1 + k)
            for r in (0, 1):
                @pl.when(not_me(i, r))
                def _(r=r):
                    s_copy(i, r, sub).start()

            return carry

        lax.fori_loop(0, heads, give_states, 0)

    local[3].wait()
    swaps[3].wait_recv()

    def make_inside(i, carry):
        scores = dot(kv[:, columns(i)], qv[:, columns(i)], ((1,), (1,))) * (1.0 / HEAD_DIM)
        start = cum_b[i]
        gaps = cum_t[i, 0:1, :] - jnp.concatenate([start] * (both // HEAD_DIM), axis=1)
        seen = lax.broadcasted_iota(jnp.int32, (both, both), 1) >= lax.broadcasted_iota(
            jnp.int32, (both, both), 0
        )
        table = jnp.where(seen, jnp.exp(jnp.where(seen, gaps, 0.0)), 0.0)
        inside[i] = dot((scores * table).astype(BF16), gv[:, columns(i)], ((1,), (0,)))
        return carry

    lax.fori_loop(0, heads, make_inside, 0)

    def scan(sub):
        at = part_of(sub)

        def scan_group(k, carry):
            group = nc - 1 - k
            for which in (0, 1):
                @pl.when(not_me(group, which))
                def _(which=which):
                    if sub == 0:
                        w_arrival(group, which).wait_recv()
                    s_arrival(group, which, sub).wait_recv()

            behind = jnp.minimum(group + 1, nc - 1)
            to_next = jnp.exp(w_in[group, 0, 2:3] + w_in[behind, 0, 1:2])
            block = s_in[group, 0, at] + jnp.exp(w_in[group, 0, 0:1]) * s_in[group, 1, at]
            a_buf[group, at] = block + to_next * a_buf[group + 1, at]
            return carry

        lax.fori_loop(0, nc, scan_group, 0)

    scan(0)

    steps = nc * SUB

    def place(p):
        return turned(lax.rem(p, nc)), lax.div(p, nc)

    def spot(p):
        group, sub = place(p)
        return group * SUB + sub

    def f_copy(p):
        return remote(f_out.at[spot(p)], f_in.at[spot(p)], f_send.at[spot(p)], f_recv.at[spot(p)], at_z(-2))

    def h_copy(p):
        return remote(h_out.at[spot(p)], h_in.at[spot(p)], h_send.at[spot(p)], h_recv.at[spot(p)], at_z(2))

    def u_copy(group, which, sub):
        return remote(
            u_out.at[which, group, part_of(sub)], u_in.at[c, part_of(sub, side * HALF)],
            u_send.at[which, group, sub], u_recv.at[c, side, sub], member(group, which),
        )

    def u_arrival(i, r, sub):
        there = u_in.at[i, part_of(sub, r * HALF)]
        return remote(there, there, u_send.at[0, 0, 0], u_recv.at[i, r, sub], member(i, r))

    def step_f(p):
        group, sub = place(p)
        pl.when(jnp.logical_not(last))(lambda: f_copy(p).wait_recv())
        own = jnp.exp(w_in[group, 0, 0:1] + w_in[group, 1, 0:1])
        f_out[spot(p)] = a_buf[group, part_of(sub)] + own * f_in[spot(p)]

        @pl.when(jnp.logical_not(first))
        def _():
            pl.when(p >= KEEP)(lambda: f_copy(p - KEEP).wait_send())
            f_copy(p).start()

    def step_h(p):
        group, sub = place(p)
        pl.when(jnp.logical_not(first))(lambda: h_copy(p).wait_recv())
        behind = jnp.minimum(group + 1, nc - 1)
        h_out[spot(p)] = h_in[spot(p)] + jnp.exp(w_in[behind, 0, 1:2]) * a_buf[group + 1, part_of(sub)]

        @pl.when(jnp.logical_not(last))
        def _():
            pl.when(p >= KEEP)(lambda: h_copy(p - KEEP).wait_send())
            h_copy(p).start()

    def step_u(p):
        group, sub = place(p)
        state = f_in[spot(p)] + jnp.exp(w_in[group, 0, 3:4]) * h_out[spot(p)]
        u_out[1, group, part_of(sub)] = state
        u_out[0, group, part_of(sub)] = (
            s_in[group, 1, part_of(sub)] * (1.0 / HEAD_DIM) + jnp.exp(w_in[group, 1, 0:1]) * state
        )

        for which in (0, 1):
            @pl.when(is_me(group, which))
            def _(which=which):
                u_in[c, part_of(sub, side * HALF)] = u_out[which, group, part_of(sub)]

            @pl.when(not_me(group, which))
            def _(which=which):
                u_copy(group, which, sub).start()

    def out_copies(i):
        at = columns(core * heads + i)
        here = pltpu.make_async_copy(out_v.at[i, mine], out_hbm.at[:, at], o_local.at[i])
        there = remote(out_v.at[i, other], out_hbm.at[:, at], o_send.at[i], o_recv.at[i], peer)
        return here, there

    def step_out(p):
        i = turned(-lax.rem(p, nc))

        @pl.when(p >= nc * (SUB - 1))
        def _():
            for r in (0, 1):
                @pl.when(not_me(i, r))
                def _(r=r):
                    for sub in range(SUB):
                        u_arrival(i, r, sub).wait_recv()

            state = u_in[i]
            high = state.astype(BF16)
            low = (state - high.astype(F32)).astype(BF16)
            keys = kv[:, columns(i)]
            carried = dot(keys, high, ((1,), (0,))) + dot(keys, low, ((1,), (0,)))
            logs = cum_b[i]
            to_end = jnp.exp(logs[both - 1 :, :] - logs)
            out_v[i] = (inside[i] + to_end * carried).astype(BF16)
            here, there = out_copies(i)
            here.start()
            there.start()

    far = jnp.maximum(pair, pairs - 1 - pair) * HOP
    plan = (
        (step_f, (pairs - 1 - pair) * HOP),
        (step_h, pair * HOP),
        (step_u, far),
        (step_out, far + LAG),
    )

    def step(t, carry):
        for sub in range(1, SUB):
            pl.when(t == sub * nc - EARLY)(functools.partial(scan, sub))
        for act, delay in plan:
            p = t - delay

            @pl.when(jnp.logical_and(p >= 0, p < steps))
            def _(act=act, p=p):
                act(p)

        return carry

    lax.fori_loop(0, far + LAG + steps, step, 0)

    def finish_chain(p, carry):
        pl.when(jnp.logical_not(first))(lambda: f_copy(p).wait_send())
        pl.when(jnp.logical_not(last))(lambda: h_copy(p).wait_send())
        return carry

    lax.fori_loop(steps - KEEP, steps, finish_chain, 0)

    def finish(i, carry):
        for r in (0, 1):
            @pl.when(not_me(i, r))
            def _(r=r):
                w_copy(i, r).wait_send()
                for sub in range(SUB):
                    s_copy(i, r, sub).wait_send()
                    u_copy(i, r, sub).wait_send()

        here, there = out_copies(i)
        here.wait()
        there.wait_send()
        there.wait_recv()
        return carry

    lax.fori_loop(0, heads, finish, 0)
    for copy in z_copies[1:] + swaps:
        copy.wait_send()


def local(dims, queries, keys, out_grad, log_decay):
    nc, nz, heads, tok = dims
    cols = heads * HEAD_DIM
    both = 2 * tok
    rows = HALF // SUB
    dma = pltpu.SemaphoreType.DMA

    def floats(*shape):
        return pltpu.VMEM(shape, F32)

    scratch = [pltpu.VMEM((both, cols), BF16)] * 3
    scratch += [
        pltpu.VMEM((2 * heads, both), BF16),
        floats(heads, both, HEAD_DIM),
        floats(heads, 8, both),
        floats(nz, heads, HEAD_DIM),
        floats(heads, 8, HEAD_DIM),
        floats(nc, 2, 8, HEAD_DIM),
        floats(heads, HEAD_DIM, HEAD_DIM),
        floats(nc, 2, HALF, HEAD_DIM),
        floats(nc + 1, HALF, HEAD_DIM),
    ]
    scratch += [floats(nc * SUB, rows, HEAD_DIM) for _ in range(4)]
    scratch += [
        floats(2, nc, HALF, HEAD_DIM),
        floats(heads, HEAD_DIM, HEAD_DIM),
        floats(heads, both, HEAD_DIM),
        pltpu.VMEM((heads, both, HEAD_DIM), BF16),
        dma((4,)), dma((4,)), dma((4,)),
        dma((nz,)), dma((nz,)),
        dma((heads, 2)), dma((nc, 2)),
        dma((heads, 2, SUB)), dma((nc, 2, SUB)),
        dma((nc * SUB,)), dma((nc * SUB,)),
        dma((nc * SUB,)), dma((nc * SUB,)),
        dma((2, nc, SUB)), dma((heads, 2, SUB)),
        dma((heads,)), dma((heads,)), dma((heads,)),
    ]
    far = pl.BlockSpec(memory_space=pltpu.HBM)
    return pl.pallas_call(
        functools.partial(kernel, dims),
        out_shape=jax.ShapeDtypeStruct(queries.shape, queries.dtype),
        in_specs=[far] * 4,
        out_specs=far,
        scratch_shapes=scratch,
        compiler_params=pltpu.CompilerParams(
            collective_id=0, has_side_effects=True, vmem_limit_bytes=VMEM_MIB * 1024 * 1024
        ),
    )(queries, keys, out_grad, log_decay.T)


def solution(mesh):
    groups, members = mesh.shape["ctx"], mesh.shape["sp"]
    placed = P(("ctx", "sp"), None)

    def run(queries, keys, out_grad, log_decay):
        dims = (groups, members // 2, log_decay.shape[1] // 2, queries.shape[0])
        return local(dims, queries, keys, out_grad, log_decay)

    return jax.shard_map(run, mesh=mesh, in_specs=(placed,) * 4, out_specs=placed, check_vma=False)
```
